32 devices in a mesh: seq: 8 (over z, y), chan: 4 (over x, core).
Axes of the slice: x: 2, y: 2, z: 4, core: 2. Of those that a mesh axis runs over, the one named last changes fastest.
Arguments:
- query_projected: bfloat16 [2048, 4096], P('seq', 'chan'), may hold values from -6 to 6
- key_stream: bfloat16 [2048, 4096], P('seq', 'chan'), may hold values from -6 to 6
- value_stream: bfloat16 [2048, 4096], P('seq', 'chan'), may hold values from -6 to 6
- short_taps: float32 [3, 3, 4096], P(None, None, 'chan'), may hold values from -3 to 3
- skip_gain: float32 [4096], P('chan'), may hold values from -4 to 4
- long_filter: float32 [2048, 4096], P('seq', 'chan'), may hold values from -4 to 4
- out_weight: bfloat16 [4096, 4096], P('chan'), may hold values from -0.09375 to 0.09375
Outputs:
- mixed: bfloat16 [2048, 4096], P('seq')
The draws below stay inside these ranges and needn't reach their ends.
All inputs are finite; a program needn't handle non-finite values.
Results may differ from the reference program's by a relative error of at most 0.005.
Values may be sent and summed in bfloat16 or wider, within the bound.
A program may use at most 128 MiB of HBM per device.

```python
import jax
import jax.numpy as jnp

EMBED_DIMENSION = 4096
SEQUENCE_EXTENT = 2048


def draw_long_filter(key, part):
    lookup_matrix = jax.random.split(key, 8)
    slow_share = 5
    slow = jax.random.randint(lookup_matrix[0], (EMBED_DIMENSION,), 0, 10) < slow_share
    fast_rate = 2.3 / jax.random.uniform(lookup_matrix[1], (EMBED_DIMENSION,), minval=30.0, maxval=50.0)
    slow_rate = 2.3 / SEQUENCE_EXTENT * jax.random.uniform(lookup_matrix[2], (EMBED_DIMENSION,), minval=0.05, maxval=0.4)
    rate = jnp.where(slow, slow_rate, fast_rate)
    lag_index = jnp.arange(SEQUENCE_EXTENT, dtype=jnp.int32)[:, None]
    lags = lag_index.astype(jnp.float32)
    envelope = jnp.exp(-rate[None, :] * lags)
    for impulse_amplitude in range(2):
        impulse_index = jax.random.randint(lookup_matrix[3 + impulse_amplitude], (EMBED_DIMENSION,), 1, SEQUENCE_EXTENT)
        falloff_factor = jax.random.uniform(lookup_matrix[5 + impulse_amplitude], (EMBED_DIMENSION,), minval=0.55, maxval=0.8)
        envelope = envelope * jnp.where(lag_index >= impulse_index[None, :], falloff_factor[None, :], 1.0)
    scale_norm = jnp.sqrt((1.0 - jnp.exp(-2.0 * rate * SEQUENCE_EXTENT)) / (1.0 - jnp.exp(-2.0 * rate)))
    noise = jnp.clip(jax.random.normal(lookup_matrix[7], (SEQUENCE_EXTENT, EMBED_DIMENSION), dtype=jnp.float32), -4.0, 4.0)
    return (noise * envelope / scale_norm[None, :]).astype(jnp.float32)


def shard_levels(key, shape, pieces, least, largest):
    level, own = 1.0, jax.random.fold_in(key, 6)
    for position, blocks in pieces:
        heights = jnp.exp(jax.random.uniform(jax.random.fold_in(own, position), (blocks,), jnp.float32, least / len(pieces), largest / len(pieces)))
        level = level * jnp.repeat(heights, shape[position] // blocks).reshape([-1 if axis == position else 1 for axis in range(len(shape))])
    return level


def bell_draw(key, extent, deviation, reach, cuts=(), kind=jnp.bfloat16):
    entries = jax.random.normal(key, extent, jnp.float32) * deviation
    if len(cuts) > 0:
        entries = shard_levels(key, extent, cuts, -0.22, 0.18) * entries
    return jnp.clip(entries, min=-reach, max=reach).astype(kind)


def setup_inputs(seed: int = 0) -> dict:
    streams_of = jax.random.split(jax.random.key(seed), 8)
    query_projected = bell_draw(streams_of[0], (SEQUENCE_EXTENT, EMBED_DIMENSION), 1.0, 6.0, ((0, 8), (1, 4)))
    key_stream = bell_draw(streams_of[1], (SEQUENCE_EXTENT, EMBED_DIMENSION), 1.0, 6.0, ((0, 8), (1, 4)))
    value_stream = bell_draw(streams_of[2], (SEQUENCE_EXTENT, EMBED_DIMENSION), 1.0, 6.0, ((0, 8), (1, 4)))
    short_taps = bell_draw(streams_of[3], (3, 3, EMBED_DIMENSION), 0.6, 3.0, ((2, 4),), jnp.float32)
    skip_gain = bell_draw(streams_of[4], (EMBED_DIMENSION,), 1.0, 4.0, ((0, 4),), jnp.float32)
    long_filter = draw_long_filter(jax.random.fold_in(streams_of[7], 71), 0)
    out_weight = bell_draw(streams_of[6], (EMBED_DIMENSION, EMBED_DIMENSION), EMBED_DIMENSION ** -0.5, 0.09375, ((0, 4),))
    return dict(query_projected=query_projected, key_stream=key_stream, value_stream=value_stream, short_taps=short_taps, skip_gain=skip_gain, long_filter=long_filter, out_weight=out_weight)


def causal_taps(field, weights):
    shift_one = jnp.concatenate([jnp.zeros_like(field[:1]), field[:-1]], axis=0)
    shift_two = jnp.concatenate([jnp.zeros_like(field[:2]), field[:-2]], axis=0)
    return weights[0] * field + weights[1] * shift_one + weights[2] * shift_two


def reference(query_projected, key_stream, value_stream, short_taps, skip_gain, long_filter, out_weight):
    shaped_q = causal_taps(query_projected.astype(jnp.float32), short_taps[:, 0])
    shaped_k = causal_taps(key_stream.astype(jnp.float32), short_taps[:, 1])
    shaped_v = causal_taps(value_stream.astype(jnp.float32), short_taps[:, 2])
    source = shaped_k * shaped_v
    padded_len = 2 * SEQUENCE_EXTENT
    product = jnp.fft.rfft(source, n=padded_len, axis=0) * jnp.fft.rfft(long_filter, n=padded_len, axis=0)
    convolved = jnp.fft.irfft(product, n=padded_len, axis=0)[:SEQUENCE_EXTENT].astype(jnp.float32)
    gated = (shaped_q * (convolved + skip_gain * source)).astype(jnp.bfloat16)
    return jnp.dot(gated, out_weight, preferred_element_type=jnp.float32).astype(jnp.bfloat16)
```

```python
import jax
import jax.numpy as jnp
import numpy as np
import ml_dtypes
from jax import lax
from jax.sharding import PartitionSpec as P


def transform(seq_len):
    period = 4 * seq_len
    freq = 2 * np.arange(seq_len, dtype=np.int64) + 1
    turns = freq[:, None] * np.arange(seq_len, dtype=np.int64)[None, :] % period
    angle = np.arange(period) * (2.0 * np.pi / period)
    table = np.stack([np.cos(angle), np.sin(angle)]).astype(ml_dtypes.bfloat16)
    return table[:, turns].reshape(2 * seq_len, seq_len)


def from_behind(array, axis, by):
    peers = lax.axis_size(axis)
    pairs = [(i, i + by) for i in range(peers) if 0 <= i + by < peers]
    return lax.ppermute(array, axis, pairs)


def on_device(
    matrix,
    query_projected,
    key_stream,
    value_stream,
    short_taps,
    skip_gain,
    long_filter,
    out_weight,
):
    shard_len, width = query_projected.shape
    seq_count = lax.axis_size("seq")
    seq_len = seq_count * shard_len
    part = width // seq_count
    streams = [query_projected, key_stream, value_stream]
    rims = from_behind(jnp.stack([x[-2:] for x in streams]), "seq", 1)

    def shape_stream(index):
        ext = jnp.concatenate([rims[index], streams[index]], axis=0).astype(jnp.float32)
        return (
            short_taps[0, index] * ext[2:]
            + short_taps[1, index] * ext[1:-1]
            + short_taps[2, index] * ext[:-2]
        )

    source = shape_stream(1) * shape_stream(2)
    fields = jnp.stack([source.astype(jnp.bfloat16), long_filter.astype(jnp.bfloat16)])
    fields = fields.reshape(2, shard_len, seq_count, part).transpose(2, 1, 0, 3)
    fields = fields.reshape(seq_count, shard_len, 2 * part)
    fields = lax.all_to_all(fields, "seq", 0, 0, tiled=True).reshape(seq_len, 2 * part)
    spec = jnp.dot(matrix, fields, preferred_element_type=jnp.float32)
    real, imag = spec[:seq_len], spec[seq_len:]
    a, b = real[:, :part], real[:, part:]
    c, d = imag[:, :part], imag[:, part:]
    prod = jnp.concatenate([a * b - c * d, a * d + c * b]) * (1.0 / seq_len)
    convolved = lax.dot_general(
        matrix,
        prod.astype(jnp.bfloat16),
        (((0,), (0,)), ((), ())),
        preferred_element_type=jnp.float32,
    ).astype(jnp.bfloat16)
    convolved = convolved.reshape(seq_count, shard_len, part)
    convolved = lax.all_to_all(convolved, "seq", 0, 0, tiled=True)
    convolved = convolved.transpose(1, 0, 2).reshape(shard_len, width).astype(jnp.float32)
    gated = (shape_stream(0) * (convolved + skip_gain * source)).astype(jnp.bfloat16)
    terms = jnp.dot(gated, out_weight, preferred_element_type=jnp.float32)
    return lax.psum(terms.astype(jnp.bfloat16), "chan")


def solution(mesh):
    mapped = jax.shard_map(
        on_device,
        mesh=mesh,
        in_specs=(
            P(None, None),
            P("seq", "chan"),
            P("seq", "chan"),
            P("seq", "chan"),
            P(None, None, "chan"),
            P("chan"),
            P("seq", "chan"),
            P("chan", None),
        ),
        out_specs=P("seq", None),
        check_vma=False,
    )

    def run(*arrays):
        return mapped(transform(arrays[0].shape[0]), *arrays)

    return run
```

```python
import functools

import jax
import jax.numpy as jnp
import numpy as np
import ml_dtypes
from jax import lax
from jax.experimental import pallas as pl
from jax.experimental.pallas import tpu as pltpu
from jax.sharding import PartitionSpec as P


def transform(seq_len):
    period = 4 * seq_len
    freq = 2 * np.arange(seq_len, dtype=np.int64) + 1
    turns = freq[:, None] * np.arange(seq_len, dtype=np.int64)[None, :] % period
    angle = np.arange(period) * (2.0 * np.pi / period)
    table = np.stack([np.cos(angle), np.sin(angle)]).astype(ml_dtypes.bfloat16)
    return table[:, turns].reshape(2 * seq_len, seq_len)


def from_behind(array, axis, by):
    peers = lax.axis_size(axis)
    pairs = [(i, i + by) for i in range(peers) if 0 <= i + by < peers]
    return lax.ppermute(array, axis, pairs)


CHUNKS = 4
MESH = pl.DeviceIdType.MESH


def project_kernel(
    rounds,
    gated_ref,
    weight_ref,
    out_ref,
    weight,
    core_send,
    core_recv,
    chip_send,
    chip_recv,
    weight_sem,
    core_send_sem,
    core_recv_sem,
    chip_send_sem,
    chip_recv_sem,
    out_send_sem,
    out_recv_sem,
):
    me = lax.axis_index("chan")
    core = lax.rem(me, 2)
    mate = me + 1 - 2 * core
    half = out_ref.shape[1] // 2
    wide = half // CHUNKS

    def chip_peer(step):
        stride = 2 << step
        return me + stride * (1 - 2 * lax.rem(me // stride, 2))

    def cols(side, j):
        return pl.ds(pl.multiple_of(side * half + j * wide, wide), wide)

    def weight_copy(turn, j):
        side = core if turn else 1 - core
        return pltpu.make_async_copy(
            weight_ref.at[:, cols(side, j)], weight.at[:, cols(side, j)], weight_sem.at[turn, j]
        )

    def core_copy(j):
        return pltpu.make_async_remote_copy(
            src_ref=core_send.at[j],
            dst_ref=core_recv.at[j],
            send_sem=core_send_sem.at[j],
            recv_sem=core_recv_sem.at[j],
            device_id={"chan": mate},
            device_id_type=MESH,
        )

    def chip_copy(step, j):
        return pltpu.make_async_remote_copy(
            src_ref=chip_send.at[step, j],
            dst_ref=chip_recv.at[step, j],
            send_sem=chip_send_sem.at[step, j],
            recv_sem=chip_recv_sem.at[step, j],
            device_id={"chan": chip_peer(step)},
            device_id_type=MESH,
        )

    def out_copy(side, j):
        return pltpu.make_async_remote_copy(
            src_ref=out_ref.at[:, cols(side, j)],
            dst_ref=out_ref.at[:, cols(side, j)],
            send_sem=out_send_sem.at[j],
            recv_sem=out_recv_sem.at[j],
            device_id={"chan": mate},
            device_id_type=MESH,
        )

    for turn in range(2):
        for j in range(CHUNKS):
            weight_copy(turn, j).start()
    barrier = pltpu.get_barrier_semaphore()
    for peer in [mate] + [chip_peer(step) for step in range(rounds)]:
        pl.semaphore_signal(barrier, inc=1, device_id={"chan": peer}, device_id_type=MESH)
    pl.semaphore_wait(barrier, 1 + rounds)

    def part(turn, j):
        weight_copy(turn, j).wait()
        side = core if turn else 1 - core
        return jnp.dot(
            gated_ref[...], weight[:, cols(side, j)], preferred_element_type=jnp.float32
        )

    @pl.loop(0, CHUNKS)
    def _(j):
        core_send[j] = part(0, j)
        core_copy(j).start()

    @pl.loop(0, CHUNKS)
    def _(j):
        own = part(1, j)
        core_copy(j).wait_recv()
        chip_send[0, j] = (own + core_recv[j]).astype(jnp.bfloat16)
        chip_copy(0, j).start()

    for step in range(rounds):

        @pl.loop(0, CHUNKS)
        def _(j):
            chip_copy(step, j).wait_recv()
            total = chip_send[step, j].astype(jnp.float32) + chip_recv[step, j].astype(jnp.float32)
            total = total.astype(jnp.bfloat16)
            if step + 1 < rounds:
                chip_send[step + 1, j] = total
                chip_copy(step + 1, j).start()
            else:
                out_ref[:, cols(core, j)] = total
                out_copy(core, j).start()

    @pl.loop(0, CHUNKS)
    def _(j):
        core_copy(j).wait_send()
        for step in range(rounds):
            chip_copy(step, j).wait_send()
        out_copy(core, j).wait_send()
        out_copy(1 - core, j).wait_recv()


def project(gated, out_weight):
    rows, depth = gated.shape
    columns = out_weight.shape[1]
    wide = columns // 2 // CHUNKS
    rounds = (lax.axis_size("chan") // 2).bit_length() - 1
    return pl.pallas_call(
        functools.partial(project_kernel, rounds),
        out_shape=jax.ShapeDtypeStruct((rows, columns), jnp.bfloat16),
        in_specs=[pl.BlockSpec(memory_space=pltpu.VMEM), pl.BlockSpec(memory_space=pl.ANY)],
        out_specs=pl.BlockSpec(memory_space=pltpu.VMEM),
        scratch_shapes=[
            pltpu.VMEM((depth, columns), jnp.bfloat16),
            pltpu.VMEM((CHUNKS, rows, wide), jnp.float32),
            pltpu.VMEM((CHUNKS, rows, wide), jnp.float32),
            pltpu.VMEM((rounds, CHUNKS, rows, wide), jnp.bfloat16),
            pltpu.VMEM((rounds, CHUNKS, rows, wide), jnp.bfloat16),
            pltpu.SemaphoreType.DMA((2, CHUNKS)),
            pltpu.SemaphoreType.DMA((CHUNKS,)),
            pltpu.SemaphoreType.DMA((CHUNKS,)),
            pltpu.SemaphoreType.DMA((rounds, CHUNKS)),
            pltpu.SemaphoreType.DMA((rounds, CHUNKS)),
            pltpu.SemaphoreType.DMA((CHUNKS,)),
            pltpu.SemaphoreType.DMA((CHUNKS,)),
        ],
        compiler_params=pltpu.CompilerParams(
            collective_id=0, has_side_effects=True, vmem_limit_bytes=32 * 2**20
        ),
        cost_estimate=pl.CostEstimate(
            flops=2 * rows * depth * columns,
            bytes_accessed=2 * depth * columns + 4 * rows * columns,
            transcendentals=0,
        ),
    )(gated, out_weight)


def on_device(
    matrix,
    query_projected,
    key_stream,
    value_stream,
    short_taps,
    skip_gain,
    long_filter,
    out_weight,
):
    shard_len, width = query_projected.shape
    seq_count = lax.axis_size("seq")
    seq_len = seq_count * shard_len
    part = width // seq_count
    streams = [query_projected, key_stream, value_stream]
    rims = from_behind(jnp.stack([x[-2:] for x in streams]), "seq", 1)

    def shape_stream(index):
        ext = jnp.concatenate([rims[index], streams[index]], axis=0).astype(jnp.float32)
        return (
            short_taps[0, index] * ext[2:]
            + short_taps[1, index] * ext[1:-1]
            + short_taps[2, index] * ext[:-2]
        )

    source = shape_stream(1) * shape_stream(2)
    fields = jnp.stack([source.astype(jnp.bfloat16), long_filter.astype(jnp.bfloat16)])
    fields = fields.reshape(2, shard_len, seq_count, part).transpose(2, 1, 0, 3)
    fields = fields.reshape(seq_count, shard_len, 2 * part)
    fields = lax.all_to_all(fields, "seq", 0, 0, tiled=True).reshape(seq_len, 2 * part)
    spec = jnp.dot(matrix, fields, preferred_element_type=jnp.float32)
    real, imag = spec[:seq_len], spec[seq_len:]
    a, b = real[:, :part], real[:, part:]
    c, d = imag[:, :part], imag[:, part:]
    prod = jnp.concatenate([a * b - c * d, a * d + c * b]) * (1.0 / seq_len)
    convolved = lax.dot_general(
        matrix,
        prod.astype(jnp.bfloat16),
        (((0,), (0,)), ((), ())),
        preferred_element_type=jnp.float32,
    ).astype(jnp.bfloat16)
    convolved = convolved.reshape(seq_count, shard_len, part)
    convolved = lax.all_to_all(convolved, "seq", 0, 0, tiled=True)
    convolved = convolved.transpose(1, 0, 2).reshape(shard_len, width).astype(jnp.float32)
    gated = (shape_stream(0) * (convolved + skip_gain * source)).astype(jnp.bfloat16)
    return project(gated, out_weight)


def solution(mesh):
    mapped = jax.shard_map(
        on_device,
        mesh=mesh,
        in_specs=(
            P(None, None),
            P("seq", "chan"),
            P("seq", "chan"),
            P("seq", "chan"),
            P(None, None, "chan"),
            P("chan"),
            P("seq", "chan"),
            P("chan", None),
        ),
        out_specs=P("seq", None),
        check_vma=False,
    )

    def run(*arrays):
        return mapped(transform(arrays[0].shape[0]), *arrays)

    return run
```

```python
import functools

import jax
import jax.numpy as jnp
import numpy as np
import ml_dtypes
from jax import lax
from jax.experimental import pallas as pl
from jax.experimental.pallas import tpu as pltpu
from jax.sharding import PartitionSpec as P


FREQS = 256
SLOTS = 4
LANES = 128


def transform(seq_len):
    period = 4 * seq_len
    freq = 2 * np.arange(seq_len // 2, dtype=np.int64) + 1
    turns = freq[:, None] * np.arange(seq_len, dtype=np.int64)[None, :] % period
    angle = np.arange(period) * (2.0 * np.pi / period)
    table = np.stack([np.cos(angle), np.sin(angle)]).astype(ml_dtypes.bfloat16)
    groups = table[:, turns].reshape(2, -1, FREQS, seq_len)
    return groups.transpose(1, 0, 2, 3).reshape(-1, 2 * FREQS, seq_len)


def from_behind(array, axis, by):
    peers = lax.axis_size(axis)
    pairs = [(i, i + by) for i in range(peers) if 0 <= i + by < peers]
    return lax.ppermute(array, axis, pairs)


CHUNKS = 4
MESH = pl.DeviceIdType.MESH


def project_kernel(
    rounds,
    gated_ref,
    weight_ref,
    out_ref,
    weight,
    core_send,
    core_recv,
    chip_send,
    chip_recv,
    weight_sem,
    core_send_sem,
    core_recv_sem,
    chip_send_sem,
    chip_recv_sem,
    out_send_sem,
    out_recv_sem,
):
    me = lax.axis_index("chan")
    core = lax.rem(me, 2)
    mate = me + 1 - 2 * core
    half = out_ref.shape[1] // 2
    wide = half // CHUNKS

    def chip_peer(step):
        stride = 2 << step
        return me + stride * (1 - 2 * lax.rem(me // stride, 2))

    def cols(side, j):
        return pl.ds(pl.multiple_of(side * half + j * wide, wide), wide)

    def weight_copy(turn, j):
        side = core if turn else 1 - core
        return pltpu.make_async_copy(
            weight_ref.at[:, cols(side, j)], weight.at[:, cols(side, j)], weight_sem.at[turn, j]
        )

    def core_copy(j):
        return pltpu.make_async_remote_copy(
            src_ref=core_send.at[j],
            dst_ref=core_recv.at[j],
            send_sem=core_send_sem.at[j],
            recv_sem=core_recv_sem.at[j],
            device_id={"chan": mate},
            device_id_type=MESH,
        )

    def chip_copy(step, j):
        return pltpu.make_async_remote_copy(
            src_ref=chip_send.at[step, j],
            dst_ref=chip_recv.at[step, j],
            send_sem=chip_send_sem.at[step, j],
            recv_sem=chip_recv_sem.at[step, j],
            device_id={"chan": chip_peer(step)},
            device_id_type=MESH,
        )

    def out_copy(side, j):
        return pltpu.make_async_remote_copy(
            src_ref=out_ref.at[:, cols(side, j)],
            dst_ref=out_ref.at[:, cols(side, j)],
            send_sem=out_send_sem.at[j],
            recv_sem=out_recv_sem.at[j],
            device_id={"chan": mate},
            device_id_type=MESH,
        )

    for turn in range(2):
        for j in range(CHUNKS):
            weight_copy(turn, j).start()
    barrier = pltpu.get_barrier_semaphore()
    for peer in [mate] + [chip_peer(step) for step in range(rounds)]:
        pl.semaphore_signal(barrier, inc=1, device_id={"chan": peer}, device_id_type=MESH)
    pl.semaphore_wait(barrier, 1 + rounds)

    def part(turn, j):
        weight_copy(turn, j).wait()
        side = core if turn else 1 - core
        return jnp.dot(
            gated_ref[...], weight[:, cols(side, j)], preferred_element_type=jnp.float32
        )

    @pl.loop(0, CHUNKS)
    def _(j):
        core_send[j] = part(0, j)
        core_copy(j).start()

    @pl.loop(0, CHUNKS)
    def _(j):
        own = part(1, j)
        core_copy(j).wait_recv()
        chip_send[0, j] = (own + core_recv[j]).astype(jnp.bfloat16)
        chip_copy(0, j).start()

    for step in range(rounds):

        @pl.loop(0, CHUNKS)
        def _(j):
            chip_copy(step, j).wait_recv()
            total = chip_send[step, j].astype(jnp.float32) + chip_recv[step, j].astype(jnp.float32)
            total = total.astype(jnp.bfloat16)
            if step + 1 < rounds:
                chip_send[step + 1, j] = total
                chip_copy(step + 1, j).start()
            else:
                out_ref[:, cols(core, j)] = total
                out_copy(core, j).start()

    @pl.loop(0, CHUNKS)
    def _(j):
        core_copy(j).wait_send()
        for step in range(rounds):
            chip_copy(step, j).wait_send()
        out_copy(core, j).wait_send()
        out_copy(1 - core, j).wait_recv()


def project(gated, out_weight):
    rows, depth = gated.shape
    columns = out_weight.shape[1]
    wide = columns // 2 // CHUNKS
    rounds = (lax.axis_size("chan") // 2).bit_length() - 1
    return pl.pallas_call(
        functools.partial(project_kernel, rounds),
        out_shape=jax.ShapeDtypeStruct((rows, columns), jnp.bfloat16),
        in_specs=[pl.BlockSpec(memory_space=pltpu.VMEM), pl.BlockSpec(memory_space=pl.ANY)],
        out_specs=pl.BlockSpec(memory_space=pltpu.VMEM),
        scratch_shapes=[
            pltpu.VMEM((depth, columns), jnp.bfloat16),
            pltpu.VMEM((CHUNKS, rows, wide), jnp.float32),
            pltpu.VMEM((CHUNKS, rows, wide), jnp.float32),
            pltpu.VMEM((rounds, CHUNKS, rows, wide), jnp.bfloat16),
            pltpu.VMEM((rounds, CHUNKS, rows, wide), jnp.bfloat16),
            pltpu.SemaphoreType.DMA((2, CHUNKS)),
            pltpu.SemaphoreType.DMA((CHUNKS,)),
            pltpu.SemaphoreType.DMA((CHUNKS,)),
            pltpu.SemaphoreType.DMA((rounds, CHUNKS)),
            pltpu.SemaphoreType.DMA((rounds, CHUNKS)),
            pltpu.SemaphoreType.DMA((CHUNKS,)),
            pltpu.SemaphoreType.DMA((CHUNKS,)),
        ],
        compiler_params=pltpu.CompilerParams(
            collective_id=1, has_side_effects=True, vmem_limit_bytes=32 * 2**20
        ),
        cost_estimate=pl.CostEstimate(
            flops=2 * rows * depth * columns,
            bytes_accessed=2 * depth * columns + 4 * rows * columns,
            transcendentals=0,
        ),
    )(gated, out_weight)


def convolve_kernel(
    fields_ref,
    matrix_ref,
    out_ref,
    fields,
    data,
    bank,
    total,
    back,
    bank_sem,
    send_sem,
    recv_sem,
    back_send_sem,
    back_recv_sem,
):
    count, shard_len, _ = fields_ref.shape
    lanes = out_ref.shape[2]
    groups, _, seq_len = matrix_ref.shape
    slots = bank.shape[0]
    me = lax.axis_index("seq")

    def bank_copy(group):
        slot = lax.rem(group, slots)
        return pltpu.make_async_copy(matrix_ref.at[group], bank.at[slot], bank_sem.at[slot])

    def there(hop):
        peer = lax.rem(me + hop, count)
        return pltpu.make_async_remote_copy(
            src_ref=fields_ref.at[peer],
            dst_ref=fields.at[me],
            send_sem=send_sem.at[hop],
            recv_sem=recv_sem.at[hop],
            device_id={"seq": peer},
            device_id_type=MESH,
        )

    def again(hop):
        peer = lax.rem(me + hop, count)
        return pltpu.make_async_remote_copy(
            src_ref=back.at[peer],
            dst_ref=out_ref.at[me],
            send_sem=back_send_sem.at[hop],
            recv_sem=back_recv_sem.at[hop],
            device_id={"seq": peer},
            device_id_type=MESH,
        )

    barrier = pltpu.get_barrier_semaphore()

    @pl.loop(1, count)
    def _(hop):
        peer = lax.rem(me + hop, count)
        pl.semaphore_signal(barrier, inc=1, device_id={"seq": peer}, device_id_type=MESH)

    pl.semaphore_wait(barrier, count - 1)

    @pl.loop(1, count)
    def _(hop):
        there(hop).start()

    @pl.loop(0, slots)
    def _(group):
        bank_copy(group).start()

    fields[me] = fields_ref[me]
    total[...] = jnp.zeros_like(total)

    @pl.loop(1, count)
    def _(hop):
        there(hop).wait_recv()

    def signs(shape, axis):
        return (1 - 2 * lax.rem(lax.broadcasted_iota(jnp.int32, shape, axis), 2)).astype(
            jnp.float32
        )

    @pl.loop(0, count)
    def _(shard):
        rows = pl.ds(pl.multiple_of(shard * shard_len, shard_len), shard_len)
        plain = fields[shard]
        data[rows, : 2 * lanes] = plain
        flipped = plain.astype(jnp.float32) * signs(plain.shape, 0)
        data[rows, 2 * lanes :] = flipped.astype(jnp.bfloat16)

    @pl.loop(0, groups)
    def _(group):
        bank_copy(group).wait()
        slot = lax.rem(group, slots)
        spec = jnp.dot(bank[slot], data[...], preferred_element_type=jnp.float32)

        def product(first):
            a, b = (spec[:FREQS, first + x : first + x + lanes] for x in (0, lanes))
            c, d = (spec[FREQS:, first + x : first + x + lanes] for x in (0, lanes))
            return jnp.concatenate([a * b - c * d, a * d + c * b]) * (1.0 / seq_len)

        prod = jnp.concatenate([product(0).T, product(2 * lanes).T]).astype(jnp.bfloat16)
        total[...] += jnp.dot(prod, bank[slot], preferred_element_type=jnp.float32)

        @pl.when(group + slots < groups)
        def _():
            bank_copy(group + slots).start()

    def block(peer):
        columns = pl.ds(pl.multiple_of(peer * shard_len, shard_len), shard_len)
        plain, flipped = total[:lanes, columns], total[lanes:, columns]
        return (plain + flipped * signs(plain.shape, 1)).T.astype(jnp.bfloat16)

    @pl.loop(1, count)
    def _(hop):
        peer = lax.rem(me + hop, count)
        back[peer] = block(peer)
        again(hop).start()

    out_ref[me] = block(me)

    @pl.loop(1, count)
    def _(hop):
        there(hop).wait_send()
        again(hop).wait()


def convolve(fields, matrix):
    count, shard_len, wide = fields.shape
    groups, rows, seq_len = matrix.shape
    slots = min(SLOTS, groups)
    lanes = wide // 2
    return pl.pallas_call(
        convolve_kernel,
        out_shape=jax.ShapeDtypeStruct((count, shard_len, lanes), jnp.bfloat16),
        in_specs=[pl.BlockSpec(memory_space=pltpu.VMEM), pl.BlockSpec(memory_space=pl.ANY)],
        out_specs=pl.BlockSpec(memory_space=pltpu.VMEM),
        scratch_shapes=[
            pltpu.VMEM((count, shard_len, wide), jnp.bfloat16),
            pltpu.VMEM((seq_len, 2 * wide), jnp.bfloat16),
            pltpu.VMEM((slots, rows, seq_len), jnp.bfloat16),
            pltpu.VMEM((wide, seq_len), jnp.float32),
            pltpu.VMEM((count, shard_len, lanes), jnp.bfloat16),
            pltpu.SemaphoreType.DMA((slots,)),
            pltpu.SemaphoreType.DMA((count,)),
            pltpu.SemaphoreType.DMA((count,)),
            pltpu.SemaphoreType.DMA((count,)),
            pltpu.SemaphoreType.DMA((count,)),
        ],
        compiler_params=pltpu.CompilerParams(
            collective_id=0, has_side_effects=True, vmem_limit_bytes=52 * 2**20
        ),
        cost_estimate=pl.CostEstimate(
            flops=12 * groups * rows * seq_len * lanes,
            bytes_accessed=2 * groups * rows * seq_len,
            transcendentals=0,
        ),
    )(fields, matrix)


def on_device(
    matrix,
    query_projected,
    key_stream,
    value_stream,
    short_taps,
    skip_gain,
    long_filter,
    out_weight,
):
    shard_len, width = query_projected.shape
    seq_count = lax.axis_size("seq")
    part = width // seq_count
    streams = [query_projected, key_stream, value_stream]
    rims = from_behind(jnp.stack([x[-2:] for x in streams]), "seq", 1)

    def shape_stream(index):
        ext = jnp.concatenate([rims[index], streams[index]], axis=0).astype(jnp.float32)
        return (
            short_taps[0, index] * ext[2:]
            + short_taps[1, index] * ext[1:-1]
            + short_taps[2, index] * ext[:-2]
        )

    source = shape_stream(1) * shape_stream(2)
    lanes = -(-part // LANES) * LANES
    fields = jnp.stack([source.astype(jnp.bfloat16), long_filter.astype(jnp.bfloat16)])
    fields = fields.reshape(2, shard_len, seq_count, part).transpose(2, 1, 0, 3)
    fields = jnp.pad(fields, ((0, 0), (0, 0), (0, 0), (0, lanes - part)))
    fields = fields.reshape(seq_count, shard_len, 2 * lanes)
    convolved = convolve(fields, matrix)[:, :, :part]
    convolved = convolved.transpose(1, 0, 2).reshape(shard_len, width).astype(jnp.float32)
    gated = (shape_stream(0) * (convolved + skip_gain * source)).astype(jnp.bfloat16)
    return project(gated, out_weight)


def solution(mesh):
    mapped = jax.shard_map(
        on_device,
        mesh=mesh,
        in_specs=(
            P(None, None, None),
            P("seq", "chan"),
            P("seq", "chan"),
            P("seq", "chan"),
            P(None, None, "chan"),
            P("chan"),
            P("seq", "chan"),
            P("chan", None),
        ),
        out_specs=P("seq", None),
        check_vma=False,
    )

    def run(*arrays):
        return mapped(transform(arrays[0].shape[0]), *arrays)

    return run
```

```python
import functools

import jax
import jax.numpy as jnp
import numpy as np
import ml_dtypes
from jax import lax
from jax.experimental import pallas as pl
from jax.experimental.pallas import tpu as pltpu
from jax.sharding import PartitionSpec as P


FREQS = 256
RIM = 16
LANES = 128


def transform(seq_len):
    period = 4 * seq_len
    freq = 2 * np.arange(seq_len // 2, dtype=np.int64) + 1
    turns = freq[:, None] * np.arange(seq_len, dtype=np.int64)[None, :] % period
    angle = np.arange(period) * (2.0 * np.pi / period)
    table = np.stack([np.cos(angle), np.sin(angle)]).astype(ml_dtypes.bfloat16)
    groups = table[:, turns].reshape(2, -1, FREQS, seq_len)
    return groups.transpose(1, 0, 2, 3).reshape(-1, 2 * FREQS, seq_len)


CHUNKS = 4
MESH = pl.DeviceIdType.MESH


def project_kernel(
    rounds,
    gated_ref,
    weight_ref,
    out_ref,
    weight,
    core_send,
    core_recv,
    chip_send,
    chip_recv,
    weight_sem,
    core_send_sem,
    core_recv_sem,
    chip_send_sem,
    chip_recv_sem,
    out_send_sem,
    out_recv_sem,
):
    me = lax.axis_index("chan")
    core = lax.rem(me, 2)
    mate = me + 1 - 2 * core
    half = out_ref.shape[1] // 2
    wide = half // CHUNKS

    def chip_peer(step):
        stride = 2 << step
        return me + stride * (1 - 2 * lax.rem(me // stride, 2))

    def cols(side, j):
        return pl.ds(pl.multiple_of(side * half + j * wide, wide), wide)

    def weight_copy(turn, j):
        side = core if turn else 1 - core
        return pltpu.make_async_copy(
            weight_ref.at[:, cols(side, j)], weight.at[:, cols(side, j)], weight_sem.at[turn, j]
        )

    def core_copy(j):
        return pltpu.make_async_remote_copy(
            src_ref=core_send.at[j],
            dst_ref=core_recv.at[j],
            send_sem=core_send_sem.at[j],
            recv_sem=core_recv_sem.at[j],
            device_id={"chan": mate},
            device_id_type=MESH,
        )

    def chip_copy(step, j):
        return pltpu.make_async_remote_copy(
            src_ref=chip_send.at[step, j],
            dst_ref=chip_recv.at[step, j],
            send_sem=chip_send_sem.at[step, j],
            recv_sem=chip_recv_sem.at[step, j],
            device_id={"chan": chip_peer(step)},
            device_id_type=MESH,
        )

    def out_copy(side, j):
        return pltpu.make_async_remote_copy(
            src_ref=out_ref.at[:, cols(side, j)],
            dst_ref=out_ref.at[:, cols(side, j)],
            send_sem=out_send_sem.at[j],
            recv_sem=out_recv_sem.at[j],
            device_id={"chan": mate},
            device_id_type=MESH,
        )

    for turn in range(2):
        for j in range(CHUNKS):
            weight_copy(turn, j).start()
    barrier = pltpu.get_barrier_semaphore()
    for peer in [mate] + [chip_peer(step) for step in range(rounds)]:
        pl.semaphore_signal(barrier, inc=1, device_id={"chan": peer}, device_id_type=MESH)
    pl.semaphore_wait(barrier, 1 + rounds)

    def part(turn, j):
        weight_copy(turn, j).wait()
        side = core if turn else 1 - core
        return jnp.dot(
            gated_ref[...], weight[:, cols(side, j)], preferred_element_type=jnp.float32
        )

    @pl.loop(0, CHUNKS)
    def _(j):
        core_send[j] = part(0, j)
        core_copy(j).start()

    @pl.loop(0, CHUNKS)
    def _(j):
        own = part(1, j)
        core_copy(j).wait_recv()
        chip_send[0, j] = (own + core_recv[j]).astype(jnp.bfloat16)
        chip_copy(0, j).start()

    for step in range(rounds):

        @pl.loop(0, CHUNKS)
        def _(j):
            chip_copy(step, j).wait_recv()
            total = chip_send[step, j].astype(jnp.float32) + chip_recv[step, j].astype(jnp.float32)
            total = total.astype(jnp.bfloat16)
            if step + 1 < rounds:
                chip_send[step + 1, j] = total
                chip_copy(step + 1, j).start()
            else:
                out_ref[:, cols(core, j)] = total
                out_copy(core, j).start()

    @pl.loop(0, CHUNKS)
    def _(j):
        core_copy(j).wait_send()
        for step in range(rounds):
            chip_copy(step, j).wait_send()
        out_copy(core, j).wait_send()
        out_copy(1 - core, j).wait_recv()


def project(gated, out_weight):
    rows, depth = gated.shape
    columns = out_weight.shape[1]
    wide = columns // 2 // CHUNKS
    rounds = (lax.axis_size("chan") // 2).bit_length() - 1
    return pl.pallas_call(
        functools.partial(project_kernel, rounds),
        out_shape=jax.ShapeDtypeStruct((rows, columns), jnp.bfloat16),
        in_specs=[pl.BlockSpec(memory_space=pltpu.VMEM), pl.BlockSpec(memory_space=pl.ANY)],
        out_specs=pl.BlockSpec(memory_space=pltpu.VMEM),
        scratch_shapes=[
            pltpu.VMEM((depth, columns), jnp.bfloat16),
            pltpu.VMEM((CHUNKS, rows, wide), jnp.float32),
            pltpu.VMEM((CHUNKS, rows, wide), jnp.float32),
            pltpu.VMEM((rounds, CHUNKS, rows, wide), jnp.bfloat16),
            pltpu.VMEM((rounds, CHUNKS, rows, wide), jnp.bfloat16),
            pltpu.SemaphoreType.DMA((2, CHUNKS)),
            pltpu.SemaphoreType.DMA((CHUNKS,)),
            pltpu.SemaphoreType.DMA((CHUNKS,)),
            pltpu.SemaphoreType.DMA((rounds, CHUNKS)),
            pltpu.SemaphoreType.DMA((rounds, CHUNKS)),
            pltpu.SemaphoreType.DMA((CHUNKS,)),
            pltpu.SemaphoreType.DMA((CHUNKS,)),
        ],
        compiler_params=pltpu.CompilerParams(
            collective_id=1, has_side_effects=True, vmem_limit_bytes=32 * 2**20
        ),
        cost_estimate=pl.CostEstimate(
            flops=2 * rows * depth * columns,
            bytes_accessed=2 * depth * columns + 4 * rows * columns,
            transcendentals=0,
        ),
    )(gated, out_weight)


def gate_kernel(
    query_ref,
    key_ref,
    value_ref,
    taps_ref,
    skip_ref,
    filter_ref,
    matrix_ref,
    gated_ref,
    rim,
    extended,
    query,
    source,
    outgoing,
    incoming,
    data,
    bank,
    filter_spec,
    total,
    back,
    convolved,
    bank_sem,
    rim_send_sem,
    rim_recv_sem,
    send_sem,
    recv_sem,
    back_send_sem,
    back_recv_sem,
):
    _, count, shard_len, lanes = outgoing.shape
    groups, _, seq_len = matrix_ref.shape
    part = query_ref.shape[1] // count
    me = lax.axis_index("seq")
    streams = (query_ref, key_ref, value_ref)

    def bank_copy(group):
        return pltpu.make_async_copy(matrix_ref.at[group], bank.at[group], bank_sem.at[group])

    def rim_copy(index):
        return pltpu.make_async_remote_copy(
            src_ref=streams[index].at[pl.ds(shard_len - RIM, RIM)],
            dst_ref=rim.at[index],
            send_sem=rim_send_sem.at[index],
            recv_sem=rim_recv_sem.at[index],
            device_id={"seq": lax.rem(me + 1, count)},
            device_id_type=MESH,
        )

    def there(field, hop):
        peer = lax.rem(me + hop, count)
        return pltpu.make_async_remote_copy(
            src_ref=outgoing.at[field, peer],
            dst_ref=incoming.at[field, me],
            send_sem=send_sem.at[field, hop],
            recv_sem=recv_sem.at[field, hop],
            device_id={"seq": peer},
            device_id_type=MESH,
        )

    def again(hop):
        peer = lax.rem(me + hop, count)
        return pltpu.make_async_remote_copy(
            src_ref=back.at[peer],
            dst_ref=convolved.at[me],
            send_sem=back_send_sem.at[hop],
            recv_sem=back_recv_sem.at[hop],
            device_id={"seq": peer},
            device_id_type=MESH,
        )

    def split(field, ref):
        if part < lanes:
            outgoing[field] = jnp.zeros(outgoing.shape[1:], outgoing.dtype)
        for peer in range(count):
            columns = ref[:, peer * part : (peer + 1) * part]
            outgoing[field, peer, :, :part] = columns.astype(jnp.bfloat16)

    def send(field):
        @pl.loop(1, count)
        def _(hop):
            there(field, hop).start()

        incoming[field, me] = outgoing[field, me]

    def signs(shape, axis):
        return (1 - 2 * lax.rem(lax.broadcasted_iota(jnp.int32, shape, axis), 2)).astype(
            jnp.float32
        )

    def receive(field):
        @pl.loop(1, count)
        def _(hop):
            there(field, hop).wait_recv()

        @pl.loop(0, count)
        def _(shard):
            rows = pl.ds(pl.multiple_of(shard * shard_len, shard_len), shard_len)
            plain = incoming[field, shard]
            data[rows, :lanes] = plain
            flipped = plain.astype(jnp.float32) * signs(plain.shape, 0)
            data[rows, lanes:] = flipped.astype(jnp.bfloat16)

    def shaped(index):
        extended[:8] = rim[index].astype(jnp.float32)[RIM - 8 :]
        extended[8:] = streams[index][...].astype(jnp.float32)
        result = taps_ref[0, index : index + 1] * extended[8:]
        for tap in (1, 2):
            rows = extended[8 - tap : 8 - tap + shard_len]
            result = result + taps_ref[tap, index : index + 1] * rows
        return result

    barrier = pltpu.get_barrier_semaphore()

    @pl.loop(1, count)
    def _(hop):
        peer = lax.rem(me + hop, count)
        pl.semaphore_signal(barrier, inc=1, device_id={"seq": peer}, device_id_type=MESH)

    split(0, filter_ref)
    pl.semaphore_wait(barrier, count - 1)

    @pl.when(me < count - 1)
    def _():
        for index in range(3):
            rim_copy(index).start()

    send(0)

    @pl.loop(0, groups)
    def _(group):
        bank_copy(group).start()

    @pl.when(me == 0)
    def _():
        rim[...] = jnp.zeros_like(rim)

    @pl.when(me > 0)
    def _():
        for index in range(3):
            rim_copy(index).wait_recv()

    source[...] = shaped(1)
    source[...] = source[...] * shaped(2)
    split(1, source)
    send(1)
    query[...] = shaped(0)
    total[...] = jnp.zeros_like(total)

    receive(0)

    @pl.loop(0, groups)
    def _(group):
        bank_copy(group).wait()
        filter_spec[group] = jnp.dot(
            bank[group], data[...], preferred_element_type=jnp.float32
        )

    receive(1)

    @pl.loop(0, groups)
    def _(group):
        spec = jnp.dot(bank[group], data[...], preferred_element_type=jnp.float32)
        a, c = spec[:FREQS], spec[FREQS:]
        b, d = filter_spec[group, :FREQS], filter_spec[group, FREQS:]
        prod = jnp.concatenate([a * b - c * d, a * d + c * b]) * (1.0 / seq_len)
        prod = jnp.concatenate([prod[:, :lanes].T, prod[:, lanes:].T]).astype(jnp.bfloat16)
        total[...] += jnp.dot(prod, bank[group], preferred_element_type=jnp.float32)

    def block(peer):
        columns = pl.ds(pl.multiple_of(peer * shard_len, shard_len), shard_len)
        plain, flipped = total[:lanes, columns], total[lanes:, columns]
        return (plain + flipped * signs(plain.shape, 1)).T.astype(jnp.bfloat16)

    @pl.loop(1, count)
    def _(hop):
        peer = lax.rem(me + hop, count)
        back[peer] = block(peer)
        again(hop).start()

    convolved[me] = block(me)

    @pl.loop(1, count)
    def _(hop):
        there(0, hop).wait_send()
        there(1, hop).wait_send()
        again(hop).wait()

    @pl.when(me < count - 1)
    def _():
        for index in range(3):
            rim_copy(index).wait_send()

    for peer in range(count):
        columns = slice(peer * part, (peer + 1) * part)
        local = convolved[peer].astype(jnp.float32)[:, :part]
        inner = local + skip_ref[:, columns] * source[:, columns]
        gated_ref[:, columns] = (query[:, columns] * inner).astype(jnp.bfloat16)


def on_device(
    matrix,
    query_projected,
    key_stream,
    value_stream,
    short_taps,
    skip_gain,
    long_filter,
    out_weight,
):
    shard_len, width = query_projected.shape
    count = lax.axis_size("seq")
    lanes = -(-(width // count) // LANES) * LANES
    groups, rows, seq_len = matrix.shape
    vmem = pl.BlockSpec(memory_space=pltpu.VMEM)
    gated = pl.pallas_call(
        gate_kernel,
        out_shape=jax.ShapeDtypeStruct((shard_len, width), jnp.bfloat16),
        in_specs=[vmem] * 6 + [pl.BlockSpec(memory_space=pl.ANY)],
        out_specs=vmem,
        scratch_shapes=[
            pltpu.VMEM((3, RIM, width), jnp.bfloat16),
            pltpu.VMEM((8 + shard_len, width), jnp.float32),
            pltpu.VMEM((shard_len, width), jnp.float32),
            pltpu.VMEM((shard_len, width), jnp.float32),
            pltpu.VMEM((2, count, shard_len, lanes), jnp.bfloat16),
            pltpu.VMEM((2, count, shard_len, lanes), jnp.bfloat16),
            pltpu.VMEM((seq_len, 2 * lanes), jnp.bfloat16),
            pltpu.VMEM((groups, rows, seq_len), jnp.bfloat16),
            pltpu.VMEM((groups, rows, 2 * lanes), jnp.float32),
            pltpu.VMEM((2 * lanes, seq_len), jnp.float32),
            pltpu.VMEM((count, shard_len, lanes), jnp.bfloat16),
            pltpu.VMEM((count, shard_len, lanes), jnp.bfloat16),
            pltpu.SemaphoreType.DMA((groups,)),
            pltpu.SemaphoreType.DMA((3,)),
            pltpu.SemaphoreType.DMA((3,)),
            pltpu.SemaphoreType.DMA((2, count)),
            pltpu.SemaphoreType.DMA((2, count)),
            pltpu.SemaphoreType.DMA((count,)),
            pltpu.SemaphoreType.DMA((count,)),
        ],
        compiler_params=pltpu.CompilerParams(
            collective_id=0,
            has_side_effects=True,
            vmem_limit_bytes=28 * 2**20 + 2 * groups * rows * seq_len,
        ),
        cost_estimate=pl.CostEstimate(
            flops=12 * groups * rows * seq_len * lanes,
            bytes_accessed=2 * groups * rows * seq_len,
            transcendentals=0,
        ),
    )(
        query_projected,
        key_stream,
        value_stream,
        short_taps,
        skip_gain[None, :],
        long_filter,
        matrix,
    )
    return project(gated, out_weight)


def solution(mesh):
    mapped = jax.shard_map(
        on_device,
        mesh=mesh,
        in_specs=(
            P(None, None, None),
            P("seq", "chan"),
            P("seq", "chan"),
            P("seq", "chan"),
            P(None, None, "chan"),
            P("chan"),
            P("seq", "chan"),
            P("chan", None),
        ),
        out_specs=P("seq", None),
        check_vma=False,
    )

    def run(*arrays):
        return mapped(transform(arrays[0].shape[0]), *arrays)

    return run
```

```python
import functools

import jax
import jax.numpy as jnp
import numpy as np
import ml_dtypes
from jax import lax
from jax.experimental import pallas as pl
from jax.experimental.pallas import tpu as pltpu
from jax.sharding import PartitionSpec as P


FREQS = 256
RIM = 16
LANES = 128


def transform(seq_len):
    period = 4 * seq_len
    freq = 2 * np.arange(seq_len // 2, dtype=np.int64) + 1
    turns = freq[:, None] * np.arange(seq_len, dtype=np.int64)[None, :] % period
    angle = np.arange(period) * (2.0 * np.pi / period)
    table = np.stack([np.cos(angle), np.sin(angle)]).astype(ml_dtypes.bfloat16)
    groups = table[:, turns].reshape(2, -1, FREQS, seq_len)
    return groups.transpose(1, 0, 2, 3).reshape(-1, 2 * FREQS, seq_len)


CHUNKS = 4
MESH = pl.DeviceIdType.MESH


def project_kernel(
    rounds,
    gated_ref,
    weight_ref,
    out_ref,
    weight,
    core_send,
    core_recv,
    chip_send,
    chip_recv,
    weight_sem,
    core_send_sem,
    core_recv_sem,
    chip_send_sem,
    chip_recv_sem,
    out_send_sem,
    out_recv_sem,
):
    me = lax.axis_index("chan")
    core = lax.rem(me, 2)
    mate = me + 1 - 2 * core
    half = out_ref.shape[1] // 2
    wide = half // CHUNKS

    def chip_peer(step):
        stride = 2 << step
        return me + stride * (1 - 2 * lax.rem(me // stride, 2))

    def cols(side, j):
        return pl.ds(pl.multiple_of(side * half + j * wide, wide), wide)

    def weight_copy(turn, j):
        side = core if turn else 1 - core
        return pltpu.make_async_copy(
            weight_ref.at[:, cols(side, j)], weight.at[:, cols(side, j)], weight_sem.at[turn, j]
        )

    def core_copy(j):
        return pltpu.make_async_remote_copy(
            src_ref=core_send.at[j],
            dst_ref=core_recv.at[j],
            send_sem=core_send_sem.at[j],
            recv_sem=core_recv_sem.at[j],
            device_id={"chan": mate},
            device_id_type=MESH,
        )

    def chip_copy(step, j):
        return pltpu.make_async_remote_copy(
            src_ref=chip_send.at[step, j],
            dst_ref=chip_recv.at[step, j],
            send_sem=chip_send_sem.at[step, j],
            recv_sem=chip_recv_sem.at[step, j],
            device_id={"chan": chip_peer(step)},
            device_id_type=MESH,
        )

    def out_copy(side, j):
        return pltpu.make_async_remote_copy(
            src_ref=out_ref.at[:, cols(side, j)],
            dst_ref=out_ref.at[:, cols(side, j)],
            send_sem=out_send_sem.at[j],
            recv_sem=out_recv_sem.at[j],
            device_id={"chan": mate},
            device_id_type=MESH,
        )

    for turn in range(2):
        for j in range(CHUNKS):
            weight_copy(turn, j).start()
    barrier = pltpu.get_barrier_semaphore()
    for peer in [mate] + [chip_peer(step) for step in range(rounds)]:
        pl.semaphore_signal(barrier, inc=1, device_id={"chan": peer}, device_id_type=MESH)
    pl.semaphore_wait(barrier, 1 + rounds)

    def part(turn, j):
        weight_copy(turn, j).wait()
        side = core if turn else 1 - core
        return jnp.dot(
            gated_ref[...], weight[:, cols(side, j)], preferred_element_type=jnp.float32
        )

    @pl.loop(0, CHUNKS)
    def _(j):
        core_send[j] = part(0, j)
        core_copy(j).start()

    @pl.loop(0, CHUNKS)
    def _(j):
        own = part(1, j)
        core_copy(j).wait_recv()
        chip_send[0, j] = (own + core_recv[j]).astype(jnp.bfloat16)
        chip_copy(0, j).start()

    for step in range(rounds):

        @pl.loop(0, CHUNKS)
        def _(j):
            chip_copy(step, j).wait_recv()
            total = chip_send[step, j].astype(jnp.float32) + chip_recv[step, j].astype(jnp.float32)
            total = total.astype(jnp.bfloat16)
            if step + 1 < rounds:
                chip_send[step + 1, j] = total
                chip_copy(step + 1, j).start()
            else:
                out_ref[:, cols(core, j)] = total
                out_copy(core, j).start()

    @pl.loop(0, CHUNKS)
    def _(j):
        core_copy(j).wait_send()
        for step in range(rounds):
            chip_copy(step, j).wait_send()
        out_copy(core, j).wait_send()
        out_copy(1 - core, j).wait_recv()


def project(gated, out_weight):
    rows, depth = gated.shape
    columns = out_weight.shape[1]
    wide = columns // 2 // CHUNKS
    rounds = (lax.axis_size("chan") // 2).bit_length() - 1
    return pl.pallas_call(
        functools.partial(project_kernel, rounds),
        out_shape=jax.ShapeDtypeStruct((rows, columns), jnp.bfloat16),
        in_specs=[pl.BlockSpec(memory_space=pltpu.VMEM), pl.BlockSpec(memory_space=pl.ANY)],
        out_specs=pl.BlockSpec(memory_space=pltpu.VMEM),
        scratch_shapes=[
            pltpu.VMEM((depth, columns), jnp.bfloat16),
            pltpu.VMEM((CHUNKS, rows, wide), jnp.float32),
            pltpu.VMEM((CHUNKS, rows, wide), jnp.float32),
            pltpu.VMEM((rounds, CHUNKS, rows, wide), jnp.bfloat16),
            pltpu.VMEM((rounds, CHUNKS, rows, wide), jnp.bfloat16),
            pltpu.SemaphoreType.DMA((2, CHUNKS)),
            pltpu.SemaphoreType.DMA((CHUNKS,)),
            pltpu.SemaphoreType.DMA((CHUNKS,)),
            pltpu.SemaphoreType.DMA((rounds, CHUNKS)),
            pltpu.SemaphoreType.DMA((rounds, CHUNKS)),
            pltpu.SemaphoreType.DMA((CHUNKS,)),
            pltpu.SemaphoreType.DMA((CHUNKS,)),
        ],
        compiler_params=pltpu.CompilerParams(
            collective_id=1, has_side_effects=True, vmem_limit_bytes=60 * 2**20
        ),
        cost_estimate=pl.CostEstimate(
            flops=2 * rows * depth * columns,
            bytes_accessed=2 * depth * columns + 4 * rows * columns,
            transcendentals=0,
        ),
    )(gated, out_weight)


def gate_kernel(
    query_ref,
    key_ref,
    value_ref,
    taps_in_ref,
    skip_in_ref,
    filter_ref,
    matrix_ref,
    gated_ref,
    held,
    taps_ref,
    skip_ref,
    rim,
    extended,
    query,
    source,
    outgoing,
    incoming,
    data,
    bank,
    filter_spec,
    total,
    back,
    convolved,
    held_sem,
    bank_sem,
    rim_send_sem,
    rim_recv_sem,
    send_sem,
    recv_sem,
    back_send_sem,
    back_recv_sem,
):
    _, count, shard_len, lanes = outgoing.shape
    groups, _, seq_len = matrix_ref.shape
    part = query_ref.shape[1] // count
    me = lax.axis_index("seq")
    streams = (query_ref, key_ref, value_ref)

    loads = [
        pltpu.make_async_copy(src, dst, held_sem.at[place])
        for place, (src, dst) in enumerate(
            [
                (filter_ref, source),
                (taps_in_ref, taps_ref),
                (key_ref, held.at[1]),
                (value_ref, held.at[2]),
                (query_ref, held.at[0]),
                (skip_in_ref, skip_ref),
            ]
        )
    ]
    for load in loads:
        load.start()

    def bank_copy(group):
        return pltpu.make_async_copy(matrix_ref.at[group], bank.at[group], bank_sem.at[group])

    def rim_copy(index):
        return pltpu.make_async_remote_copy(
            src_ref=streams[index].at[pl.ds(shard_len - RIM, RIM)],
            dst_ref=rim.at[index],
            send_sem=rim_send_sem.at[index],
            recv_sem=rim_recv_sem.at[index],
            device_id={"seq": lax.rem(me + 1, count)},
            device_id_type=MESH,
        )

    def there(field, hop):
        peer = lax.rem(me + hop, count)
        return pltpu.make_async_remote_copy(
            src_ref=outgoing.at[field, peer],
            dst_ref=incoming.at[field, me],
            send_sem=send_sem.at[field, hop],
            recv_sem=recv_sem.at[field, hop],
            device_id={"seq": peer},
            device_id_type=MESH,
        )

    def again(hop):
        peer = lax.rem(me + hop, count)
        return pltpu.make_async_remote_copy(
            src_ref=back.at[peer],
            dst_ref=convolved.at[me],
            send_sem=back_send_sem.at[hop],
            recv_sem=back_recv_sem.at[hop],
            device_id={"seq": peer},
            device_id_type=MESH,
        )

    def split(field, ref):
        if part < lanes:
            outgoing[field] = jnp.zeros(outgoing.shape[1:], outgoing.dtype)
        for peer in range(count):
            columns = ref[:, peer * part : (peer + 1) * part]
            outgoing[field, peer, :, :part] = columns.astype(jnp.bfloat16)

    def send(field):
        @pl.loop(1, count)
        def _(hop):
            there(field, hop).start()

        incoming[field, me] = outgoing[field, me]

    def signs(shape, axis):
        return (1 - 2 * lax.rem(lax.broadcasted_iota(jnp.int32, shape, axis), 2)).astype(
            jnp.float32
        )

    def receive(field):
        @pl.loop(1, count)
        def _(hop):
            there(field, hop).wait_recv()

        @pl.loop(0, count)
        def _(shard):
            rows = pl.ds(pl.multiple_of(shard * shard_len, shard_len), shard_len)
            plain = incoming[field, shard]
            data[rows, :lanes] = plain
            flipped = plain.astype(jnp.float32) * signs(plain.shape, 0)
            data[rows, lanes:] = flipped.astype(jnp.bfloat16)

    def shaped(index):
        extended[:8] = rim[index].astype(jnp.float32)[RIM - 8 :]
        extended[8:] = held[index].astype(jnp.float32)
        result = taps_ref[0, index : index + 1] * extended[8:]
        for tap in (1, 2):
            rows = extended[8 - tap : 8 - tap + shard_len]
            result = result + taps_ref[tap, index : index + 1] * rows
        return result

    barrier = pltpu.get_barrier_semaphore()

    @pl.loop(1, count)
    def _(hop):
        peer = lax.rem(me + hop, count)
        pl.semaphore_signal(barrier, inc=1, device_id={"seq": peer}, device_id_type=MESH)

    loads[0].wait()
    split(0, source)
    pl.semaphore_wait(barrier, count - 1)

    @pl.when(me < count - 1)
    def _():
        for index in range(3):
            rim_copy(index).start()

    send(0)

    @pl.loop(0, groups)
    def _(group):
        bank_copy(group).start()

    @pl.when(me == 0)
    def _():
        rim[...] = jnp.zeros_like(rim)

    @pl.when(me > 0)
    def _():
        for index in range(3):
            rim_copy(index).wait_recv()

    for load in loads[1:]:
        load.wait()
    source[...] = shaped(1)
    source[...] = source[...] * shaped(2)
    split(1, source)
    send(1)
    query[...] = shaped(0)
    total[...] = jnp.zeros_like(total)

    receive(0)

    @pl.loop(0, groups)
    def _(group):
        bank_copy(group).wait()
        filter_spec[group] = jnp.dot(
            bank[group], data[...], preferred_element_type=jnp.float32
        )

    receive(1)

    @pl.loop(0, groups)
    def _(group):
        spec = jnp.dot(bank[group], data[...], preferred_element_type=jnp.float32)
        a, c = spec[:FREQS], spec[FREQS:]
        b, d = filter_spec[group, :FREQS], filter_spec[group, FREQS:]
        prod = jnp.concatenate([a * b - c * d, a * d + c * b]) * (1.0 / seq_len)
        prod = jnp.concatenate([prod[:, :lanes].T, prod[:, lanes:].T]).astype(jnp.bfloat16)
        total[...] += jnp.dot(prod, bank[group], preferred_element_type=jnp.float32)

    def block(peer):
        columns = pl.ds(pl.multiple_of(peer * shard_len, shard_len), shard_len)
        plain, flipped = total[:lanes, columns], total[lanes:, columns]
        return (plain + flipped * signs(plain.shape, 1)).T.astype(jnp.bfloat16)

    @pl.loop(1, count)
    def _(hop):
        peer = lax.rem(me + hop, count)
        back[peer] = block(peer)
        again(hop).start()

    convolved[me] = block(me)

    @pl.loop(1, count)
    def _(hop):
        there(0, hop).wait_send()
        there(1, hop).wait_send()
        again(hop).wait()

    @pl.when(me < count - 1)
    def _():
        for index in range(3):
            rim_copy(index).wait_send()

    for peer in range(count):
        columns = slice(peer * part, (peer + 1) * part)
        local = convolved[peer].astype(jnp.float32)[:, :part]
        inner = local + skip_ref[:, columns] * source[:, columns]
        gated_ref[:, columns] = (query[:, columns] * inner).astype(jnp.bfloat16)


def on_device(
    matrix,
    query_projected,
    key_stream,
    value_stream,
    short_taps,
    skip_gain,
    long_filter,
    out_weight,
):
    shard_len, width = query_projected.shape
    count = lax.axis_size("seq")
    lanes = -(-(width // count) // LANES) * LANES
    groups, rows, seq_len = matrix.shape
    vmem = pl.BlockSpec(memory_space=pltpu.VMEM)
    gated = pl.pallas_call(
        gate_kernel,
        out_shape=jax.ShapeDtypeStruct((shard_len, width), jnp.bfloat16),
        in_specs=[pl.BlockSpec(memory_space=pl.ANY)] * 7,
        out_specs=vmem,
        scratch_shapes=[
            pltpu.VMEM((3, shard_len, width), jnp.bfloat16),
            pltpu.VMEM(short_taps.shape, jnp.float32),
            pltpu.VMEM((1, width), jnp.float32),
            pltpu.VMEM((3, RIM, width), jnp.bfloat16),
            pltpu.VMEM((8 + shard_len, width), jnp.float32),
            pltpu.VMEM((shard_len, width), jnp.float32),
            pltpu.VMEM((shard_len, width), jnp.float32),
            pltpu.VMEM((2, count, shard_len, lanes), jnp.bfloat16),
            pltpu.VMEM((2, count, shard_len, lanes), jnp.bfloat16),
            pltpu.VMEM((seq_len, 2 * lanes), jnp.bfloat16),
            pltpu.VMEM((groups, rows, seq_len), jnp.bfloat16),
            pltpu.VMEM((groups, rows, 2 * lanes), jnp.float32),
            pltpu.VMEM((2 * lanes, seq_len), jnp.float32),
            pltpu.VMEM((count, shard_len, lanes), jnp.bfloat16),
            pltpu.VMEM((count, shard_len, lanes), jnp.bfloat16),
            pltpu.SemaphoreType.DMA((6,)),
            pltpu.SemaphoreType.DMA((groups,)),
            pltpu.SemaphoreType.DMA((3,)),
            pltpu.SemaphoreType.DMA((3,)),
            pltpu.SemaphoreType.DMA((2, count)),
            pltpu.SemaphoreType.DMA((2, count)),
            pltpu.SemaphoreType.DMA((count,)),
            pltpu.SemaphoreType.DMA((count,)),
        ],
        compiler_params=pltpu.CompilerParams(
            collective_id=0,
            has_side_effects=True,
            vmem_limit_bytes=60 * 2**20,
        ),
        cost_estimate=pl.CostEstimate(
            flops=12 * groups * rows * seq_len * lanes,
            bytes_accessed=2 * groups * rows * seq_len,
            transcendentals=0,
        ),
    )(
        query_projected,
        key_stream,
        value_stream,
        short_taps,
        skip_gain[None, :],
        long_filter,
        matrix,
    )
    return project(gated, out_weight)


def solution(mesh):
    mapped = jax.shard_map(
        on_device,
        mesh=mesh,
        in_specs=(
            P(None, None, None),
            P("seq", "chan"),
            P("seq", "chan"),
            P("seq", "chan"),
            P(None, None, "chan"),
            P("chan"),
            P("seq", "chan"),
            P("chan", None),
        ),
        out_specs=P("seq", None),
        check_vma=False,
    )

    def run(*arrays):
        return mapped(transform(arrays[0].shape[0]), *arrays)

    return run
```

```python
import functools

import jax
import jax.numpy as jnp
import numpy as np
import ml_dtypes
from jax import lax
from jax.experimental import pallas as pl
from jax.experimental.pallas import tpu as pltpu
from jax.sharding import PartitionSpec as P


FREQS = 256
RIM = 16
LANES = 128


def transform(seq_len):
    period = 4 * seq_len
    freq = 2 * np.arange(seq_len // 2, dtype=np.int64) + 1
    turns = freq[:, None] * np.arange(seq_len, dtype=np.int64)[None, :] % period
    angle = np.arange(period) * (2.0 * np.pi / period)
    table = np.stack([np.cos(angle), np.sin(angle)]).astype(ml_dtypes.bfloat16)
    groups = table[:, turns].reshape(2, -1, FREQS, seq_len)
    return groups.transpose(1, 0, 2, 3).reshape(-1, 2 * FREQS, seq_len)


CHUNKS = 8
MESH = pl.DeviceIdType.MESH


def project_kernel(
    rounds,
    gated_ref,
    weight_ref,
    out_ref,
    weight,
    core_send,
    core_recv,
    chip_send,
    chip_recv,
    weight_sem,
    core_send_sem,
    core_recv_sem,
    chip_send_sem,
    chip_recv_sem,
    out_send_sem,
    out_recv_sem,
):
    me = lax.axis_index("chan")
    core = lax.rem(me, 2)
    mate = me + 1 - 2 * core
    half = out_ref.shape[1] // 2
    wide = half // CHUNKS

    def chip_peer(step):
        stride = 2 << step
        return me + stride * (1 - 2 * lax.rem(me // stride, 2))

    def cols(side, j):
        return pl.ds(pl.multiple_of(side * half + j * wide, wide), wide)

    def weight_copy(turn, j):
        side = core if turn else 1 - core
        return pltpu.make_async_copy(
            weight_ref.at[:, cols(side, j)], weight.at[:, cols(side, j)], weight_sem.at[turn, j]
        )

    def core_copy(j):
        return pltpu.make_async_remote_copy(
            src_ref=core_send.at[j],
            dst_ref=core_recv.at[j],
            send_sem=core_send_sem.at[j],
            recv_sem=core_recv_sem.at[j],
            device_id={"chan": mate},
            device_id_type=MESH,
        )

    def chip_copy(step, j):
        return pltpu.make_async_remote_copy(
            src_ref=chip_send.at[step, j],
            dst_ref=chip_recv.at[step, j],
            send_sem=chip_send_sem.at[step, j],
            recv_sem=chip_recv_sem.at[step, j],
            device_id={"chan": chip_peer(step)},
            device_id_type=MESH,
        )

    def out_copy(side, j):
        return pltpu.make_async_remote_copy(
            src_ref=out_ref.at[:, cols(side, j)],
            dst_ref=out_ref.at[:, cols(side, j)],
            send_sem=out_send_sem.at[j],
            recv_sem=out_recv_sem.at[j],
            device_id={"chan": mate},
            device_id_type=MESH,
        )

    for j in range(CHUNKS):
        for turn in range(2):
            weight_copy(turn, j).start()
    barrier = pltpu.get_barrier_semaphore()
    for peer in [mate] + [chip_peer(step) for step in range(rounds)]:
        pl.semaphore_signal(barrier, inc=1, device_id={"chan": peer}, device_id_type=MESH)
    pl.semaphore_wait(barrier, 1 + rounds)

    def part(turn, j):
        weight_copy(turn, j).wait()
        side = core if turn else 1 - core
        return jnp.dot(
            gated_ref[...], weight[:, cols(side, j)], preferred_element_type=jnp.float32
        )

    def give(j):
        core_send[j] = part(0, j)
        core_copy(j).start()

    give(0)

    @pl.loop(0, CHUNKS)
    def _(j):
        @pl.when(j + 1 < CHUNKS)
        def _():
            give(j + 1)

        own = part(1, j)
        core_copy(j).wait_recv()
        chip_send[0, j] = (own + core_recv[j]).astype(jnp.bfloat16)
        chip_copy(0, j).start()

    for step in range(rounds):

        @pl.loop(0, CHUNKS)
        def _(j):
            chip_copy(step, j).wait_recv()
            total = chip_send[step, j].astype(jnp.float32) + chip_recv[step, j].astype(jnp.float32)
            total = total.astype(jnp.bfloat16)
            if step + 1 < rounds:
                chip_send[step + 1, j] = total
                chip_copy(step + 1, j).start()
            else:
                out_ref[:, cols(core, j)] = total
                out_copy(core, j).start()

    @pl.loop(0, CHUNKS)
    def _(j):
        core_copy(j).wait_send()
        for step in range(rounds):
            chip_copy(step, j).wait_send()
        out_copy(core, j).wait_send()
        out_copy(1 - core, j).wait_recv()


def project(gated, out_weight):
    rows, depth = gated.shape
    columns = out_weight.shape[1]
    wide = columns // 2 // CHUNKS
    rounds = (lax.axis_size("chan") // 2).bit_length() - 1
    return pl.pallas_call(
        functools.partial(project_kernel, rounds),
        out_shape=jax.ShapeDtypeStruct((rows, columns), jnp.bfloat16),
        in_specs=[pl.BlockSpec(memory_space=pltpu.VMEM), pl.BlockSpec(memory_space=pl.ANY)],
        out_specs=pl.BlockSpec(memory_space=pltpu.VMEM),
        scratch_shapes=[
            pltpu.VMEM((depth, columns), jnp.bfloat16),
            pltpu.VMEM((CHUNKS, rows, wide), jnp.float32),
            pltpu.VMEM((CHUNKS, rows, wide), jnp.float32),
            pltpu.VMEM((rounds, CHUNKS, rows, wide), jnp.bfloat16),
            pltpu.VMEM((rounds, CHUNKS, rows, wide), jnp.bfloat16),
            pltpu.SemaphoreType.DMA((2, CHUNKS)),
            pltpu.SemaphoreType.DMA((CHUNKS,)),
            pltpu.SemaphoreType.DMA((CHUNKS,)),
            pltpu.SemaphoreType.DMA((rounds, CHUNKS)),
            pltpu.SemaphoreType.DMA((rounds, CHUNKS)),
            pltpu.SemaphoreType.DMA((CHUNKS,)),
            pltpu.SemaphoreType.DMA((CHUNKS,)),
        ],
        compiler_params=pltpu.CompilerParams(
            collective_id=1, has_side_effects=True, vmem_limit_bytes=60 * 2**20
        ),
        cost_estimate=pl.CostEstimate(
            flops=2 * rows * depth * columns,
            bytes_accessed=2 * depth * columns + 4 * rows * columns,
            transcendentals=0,
        ),
    )(gated, out_weight)


def gate_kernel(
    query_ref,
    key_ref,
    value_ref,
    taps_in_ref,
    skip_in_ref,
    filter_ref,
    matrix_ref,
    gated_ref,
    held,
    taps_ref,
    skip_ref,
    rim,
    extended,
    query,
    source,
    outgoing,
    incoming,
    data,
    bank,
    filter_spec,
    total,
    back,
    convolved,
    held_sem,
    bank_sem,
    rim_send_sem,
    rim_recv_sem,
    send_sem,
    recv_sem,
    back_send_sem,
    back_recv_sem,
):
    _, count, shard_len, lanes = outgoing.shape
    groups, _, seq_len = matrix_ref.shape
    part = query_ref.shape[1] // count
    me = lax.axis_index("seq")
    streams = (query_ref, key_ref, value_ref)

    loads = [
        pltpu.make_async_copy(src, dst, held_sem.at[place])
        for place, (src, dst) in enumerate(
            [
                (filter_ref, source),
                (taps_in_ref, taps_ref),
                (key_ref, held.at[1]),
                (value_ref, held.at[2]),
                (query_ref, held.at[0]),
                (skip_in_ref, skip_ref),
            ]
        )
    ]
    for load in loads:
        load.start()

    def bank_copy(group):
        return pltpu.make_async_copy(matrix_ref.at[group], bank.at[group], bank_sem.at[group])

    def rim_copy(index):
        return pltpu.make_async_remote_copy(
            src_ref=streams[index].at[pl.ds(shard_len - RIM, RIM)],
            dst_ref=rim.at[index],
            send_sem=rim_send_sem.at[index],
            recv_sem=rim_recv_sem.at[index],
            device_id={"seq": lax.rem(me + 1, count)},
            device_id_type=MESH,
        )

    def there(field, hop):
        peer = lax.rem(me + hop, count)
        return pltpu.make_async_remote_copy(
            src_ref=outgoing.at[field, peer],
            dst_ref=incoming.at[field, me],
            send_sem=send_sem.at[field, hop],
            recv_sem=recv_sem.at[field, hop],
            device_id={"seq": peer},
            device_id_type=MESH,
        )

    def again(hop):
        peer = lax.rem(me + hop, count)
        return pltpu.make_async_remote_copy(
            src_ref=back.at[peer],
            dst_ref=convolved.at[me],
            send_sem=back_send_sem.at[hop],
            recv_sem=back_recv_sem.at[hop],
            device_id={"seq": peer},
            device_id_type=MESH,
        )

    def split(field, ref):
        if part < lanes:
            outgoing[field] = jnp.zeros(outgoing.shape[1:], outgoing.dtype)
        for peer in range(count):
            columns = ref[:, peer * part : (peer + 1) * part]
            outgoing[field, peer, :, :part] = columns.astype(jnp.bfloat16)

    def send(field):
        @pl.loop(1, count)
        def _(hop):
            there(field, hop).start()

        incoming[field, me] = outgoing[field, me]

    def signs(shape, axis):
        return (1 - 2 * lax.rem(lax.broadcasted_iota(jnp.int32, shape, axis), 2)).astype(
            jnp.float32
        )

    def receive(field):
        @pl.loop(1, count)
        def _(hop):
            there(field, hop).wait_recv()

        @pl.loop(0, count)
        def _(shard):
            rows = pl.ds(pl.multiple_of(shard * shard_len, shard_len), shard_len)
            plain = incoming[field, shard]
            data[rows, :lanes] = plain
            flipped = plain.astype(jnp.float32) * signs(plain.shape, 0)
            data[rows, lanes:] = flipped.astype(jnp.bfloat16)

    def shaped(index):
        extended[:8] = rim[index].astype(jnp.float32)[RIM - 8 :]
        extended[8:] = held[index].astype(jnp.float32)
        result = taps_ref[0, index : index + 1] * extended[8:]
        for tap in (1, 2):
            rows = extended[8 - tap : 8 - tap + shard_len]
            result = result + taps_ref[tap, index : index + 1] * rows
        return result

    barrier = pltpu.get_barrier_semaphore()

    @pl.loop(1, count)
    def _(hop):
        peer = lax.rem(me + hop, count)
        pl.semaphore_signal(barrier, inc=1, device_id={"seq": peer}, device_id_type=MESH)

    loads[0].wait()
    split(0, source)
    pl.semaphore_wait(barrier, count - 1)

    @pl.when(me < count - 1)
    def _():
        for index in range(3):
            rim_copy(index).start()

    send(0)

    @pl.loop(0, groups)
    def _(group):
        bank_copy(group).start()

    @pl.when(me == 0)
    def _():
        rim[...] = jnp.zeros_like(rim)

    @pl.when(me > 0)
    def _():
        for index in range(3):
            rim_copy(index).wait_recv()

    for load in loads[1:]:
        load.wait()
    source[...] = shaped(1)
    source[...] = source[...] * shaped(2)
    split(1, source)
    send(1)
    query[...] = shaped(0)
    total[...] = jnp.zeros_like(total)

    receive(0)

    @pl.loop(0, groups)
    def _(group):
        bank_copy(group).wait()
        filter_spec[group] = jnp.dot(
            bank[group], data[...], preferred_element_type=jnp.float32
        )

    receive(1)

    @pl.loop(0, groups)
    def _(group):
        spec = jnp.dot(bank[group], data[...], preferred_element_type=jnp.float32)
        a, c = spec[:FREQS], spec[FREQS:]
        b, d = filter_spec[group, :FREQS], filter_spec[group, FREQS:]
        prod = jnp.concatenate([a * b - c * d, a * d + c * b]) * (1.0 / seq_len)
        prod = jnp.concatenate([prod[:, :lanes].T, prod[:, lanes:].T]).astype(jnp.bfloat16)
        total[...] += jnp.dot(prod, bank[group], preferred_element_type=jnp.float32)

    def block(peer):
        columns = pl.ds(pl.multiple_of(peer * shard_len, shard_len), shard_len)
        plain, flipped = total[:lanes, columns], total[lanes:, columns]
        return (plain + flipped * signs(plain.shape, 1)).T.astype(jnp.bfloat16)

    @pl.loop(1, count)
    def _(hop):
        peer = lax.rem(me + hop, count)
        back[peer] = block(peer)
        again(hop).start()

    convolved[me] = block(me)

    @pl.loop(1, count)
    def _(hop):
        there(0, hop).wait_send()
        there(1, hop).wait_send()
        again(hop).wait()

    @pl.when(me < count - 1)
    def _():
        for index in range(3):
            rim_copy(index).wait_send()

    for peer in range(count):
        columns = slice(peer * part, (peer + 1) * part)
        local = convolved[peer].astype(jnp.float32)[:, :part]
        inner = local + skip_ref[:, columns] * source[:, columns]
        gated_ref[:, columns] = (query[:, columns] * inner).astype(jnp.bfloat16)


def on_device(
    matrix,
    query_projected,
    key_stream,
    value_stream,
    short_taps,
    skip_gain,
    long_filter,
    out_weight,
):
    shard_len, width = query_projected.shape
    count = lax.axis_size("seq")
    lanes = -(-(width // count) // LANES) * LANES
    groups, rows, seq_len = matrix.shape
    vmem = pl.BlockSpec(memory_space=pltpu.VMEM)
    gated = pl.pallas_call(
        gate_kernel,
        out_shape=jax.ShapeDtypeStruct((shard_len, width), jnp.bfloat16),
        in_specs=[pl.BlockSpec(memory_space=pl.ANY)] * 7,
        out_specs=vmem,
        scratch_shapes=[
            pltpu.VMEM((3, shard_len, width), jnp.bfloat16),
            pltpu.VMEM(short_taps.shape, jnp.float32),
            pltpu.VMEM((1, width), jnp.float32),
            pltpu.VMEM((3, RIM, width), jnp.bfloat16),
            pltpu.VMEM((8 + shard_len, width), jnp.float32),
            pltpu.VMEM((shard_len, width), jnp.float32),
            pltpu.VMEM((shard_len, width), jnp.float32),
            pltpu.VMEM((2, count, shard_len, lanes), jnp.bfloat16),
            pltpu.VMEM((2, count, shard_len, lanes), jnp.bfloat16),
            pltpu.VMEM((seq_len, 2 * lanes), jnp.bfloat16),
            pltpu.VMEM((groups, rows, seq_len), jnp.bfloat16),
            pltpu.VMEM((groups, rows, 2 * lanes), jnp.float32),
            pltpu.VMEM((2 * lanes, seq_len), jnp.float32),
            pltpu.VMEM((count, shard_len, lanes), jnp.bfloat16),
            pltpu.VMEM((count, shard_len, lanes), jnp.bfloat16),
            pltpu.SemaphoreType.DMA((6,)),
            pltpu.SemaphoreType.DMA((groups,)),
            pltpu.SemaphoreType.DMA((3,)),
            pltpu.SemaphoreType.DMA((3,)),
            pltpu.SemaphoreType.DMA((2, count)),
            pltpu.SemaphoreType.DMA((2, count)),
            pltpu.SemaphoreType.DMA((count,)),
            pltpu.SemaphoreType.DMA((count,)),
        ],
        compiler_params=pltpu.CompilerParams(
            collective_id=0,
            has_side_effects=True,
            vmem_limit_bytes=60 * 2**20,
        ),
        cost_estimate=pl.CostEstimate(
            flops=12 * groups * rows * seq_len * lanes,
            bytes_accessed=2 * groups * rows * seq_len,
            transcendentals=0,
        ),
    )(
        query_projected,
        key_stream,
        value_stream,
        short_taps,
        skip_gain[None, :],
        long_filter,
        matrix,
    )
    return project(gated, out_weight)


def solution(mesh):
    mapped = jax.shard_map(
        on_device,
        mesh=mesh,
        in_specs=(
            P(None, None, None),
            P("seq", "chan"),
            P("seq", "chan"),
            P("seq", "chan"),
            P(None, None, "chan"),
            P("chan"),
            P("seq", "chan"),
            P("chan", None),
        ),
        out_specs=P("seq", None),
        check_vma=False,
    )

    def run(*arrays):
        return mapped(transform(arrays[0].shape[0]), *arrays)

    return run
```
